32 devices in a mesh: dom: 8 (over z, x), cls: 4 (over y, core).
Axes of the slice: x: 2, y: 2, z: 4, core: 2. Of those that a mesh axis runs over, the one named last changes fastest.
Arguments:
- particles: bfloat16 [256, 128, 9, 128], P(None, ('dom', 'cls')), may hold values from -6 to 6
- references: bfloat16 [256, 200, 128], P(None, 'cls'), may hold values from -6 to 6
- class_ids: int32 [128, 3], P(('dom', 'cls')), may hold values from 0 to 199, all different within a row
- counts: int32 [128], P(('dom', 'cls')), may hold values from 1 to 3
- shift_ids: int32 [128, 3], P(('dom', 'cls')), may hold values from 0 to 8
- weights: bfloat16 [128, 3], P(('dom', 'cls')), may hold values from 0.049804688 to 1
Outputs:
- best_scores: float32 [128, 200], P('dom', 'cls')
- class_means: float32 [256, 200, 128], P('dom', 'cls')
The draws below stay inside these ranges and needn't reach their ends.
Inputs may be any that keep to these rules, and one draw needn't show every extreme that they name: `class_ids`: each particle's row names 3 different classes and every class is named by some row; only the first counts entries of a row are significant.
All inputs are finite; a program needn't handle non-finite values.
Results may differ from the reference program's by a relative error of at most 0.0012.
Values may be sent and summed in bfloat16 or wider, within the bound.
A program may use at most 128 MiB of HBM per device.

```python
import math
import jax
import jax.numpy as jnp
from jax import lax

CYCLES = 64
ANGLES = 256
SHIFTS = 9
SIGNIF = 3
CLASSES = 200
PARTICLES = 128


def set_ends(entries, key, low, largest):
    shape = entries.shape
    spot = [jax.random.randint(jax.random.fold_in(key, axis), (), 0, shape[axis]) for axis in range(len(shape))]
    entries = entries.at[tuple(spot)].set(low)
    longest = shape.index(max(shape))
    spot[longest] = (spot[longest] + 1) % shape[longest]
    return entries.at[tuple(spot)].set(largest)


def level_of(own_key, extent, split, low, high):
    factor_of, own = 1.0, jax.random.fold_in(own_key, 6)
    for dim, parts in split:
        draws = jnp.exp(jax.random.uniform(jax.random.fold_in(own, dim), (parts,), jnp.float32, low / len(split), high / len(split)))
        factor_of = factor_of * jnp.repeat(draws, extent[dim] // parts).reshape([-1 if axis == dim else 1 for axis in range(len(extent))])
    return factor_of


def picks_of(rng, rows, number_of, top, lift):
    order = jax.random.permutation(jax.random.fold_in(rng, 1), number_of)
    favour = order
    for power in range(3):
        favour = favour * favour // number_of
    favour = favour * lift // number_of
    chance = jax.random.randint(jax.random.fold_in(rng, 2), (rows, number_of), 0, 4096) + favour
    fixed_rows = jax.random.permutation(jax.random.fold_in(rng, 3), rows)[jnp.arange(number_of) % rows]
    chance = jnp.where(jnp.arange(rows)[:, None] == fixed_rows[None, :], 1 << 14, chance)
    merit = chance * number_of + jnp.arange(number_of)
    return lax.top_k(merit.astype(jnp.int32), top)[1].astype(jnp.int32)


def noise(rng, shape, scale, most, split=(), kind=jnp.bfloat16):
    array = jax.random.normal(rng, shape, jnp.float32) * scale
    if len(split) > 0:
        array = level_of(rng, shape, split, -0.22, 0.18) * array
    return jnp.clip(array, min=-most, max=most).astype(kind)


def setup_inputs(seed: int = 0) -> dict:
    seeds = jax.random.split(jax.random.key(seed), 7)
    particles = noise(seeds[0], (ANGLES, PARTICLES, SHIFTS, 2 * CYCLES), 1.0, 6.0, ((1, 32),))
    references = noise(seeds[1], (ANGLES, CLASSES, 2 * CYCLES), 1.0, 6.0, ((1, 4),))
    class_ids = picks_of(seeds[2], PARTICLES, CLASSES, SIGNIF, 245)
    counts = set_ends(jax.random.randint(seeds[3], (PARTICLES,), 1, SIGNIF + 1), jax.random.fold_in(seeds[3], 1), 1, SIGNIF).astype(jnp.int32)
    shift_ids = set_ends(jax.random.randint(seeds[4], (PARTICLES, SIGNIF), 0, SHIFTS), jax.random.fold_in(seeds[4], 1), 0, SHIFTS - 1).astype(jnp.int32)
    weights = jnp.clip(jnp.exp(math.log(1.0) - 2.9996462 * jax.random.uniform(seeds[5], (PARTICLES, SIGNIF), jnp.float32) ** level_of(seeds[5], (PARTICLES, SIGNIF), ((0, 32),), -0.2, 0.2)), 0.049804688, 1.0).astype(jnp.bfloat16)
    return dict(particles=particles, references=references, class_ids=class_ids, counts=counts, shift_ids=shift_ids, weights=weights)


def angle_table(angles):
    harmonic = jnp.arange(angles, dtype=jnp.int32)
    product = harmonic[:, None] * harmonic[None, :] % angles
    phase_angle = product.astype(jnp.float32) * (2.0 * math.pi / angles)
    return jnp.stack([jnp.cos(phase_angle), -jnp.sin(phase_angle)]).astype(jnp.bfloat16)

def real_form(references, cycles):
    real_part = references[:, :, :cycles]
    imag_part = references[:, :, cycles:]
    swapped = jnp.concatenate([-imag_part, real_part], axis=2)
    return jnp.concatenate([references, swapped], axis=1)

def reference(particles, references, class_ids, counts, shift_ids, weights):
    table_wide = angle_table(ANGLES).astype(jnp.float32)
    stacked = real_form(references, CYCLES).astype(jnp.float32)
    scale = 1.0 / math.sqrt(2.0 * CYCLES * ANGLES)

    def score_one(image):
        products = jnp.einsum('msc,mqc->sqm', image.astype(jnp.float32), stacked)
        rounded = products.astype(jnp.bfloat16).astype(jnp.float32)
        rounded = rounded.reshape(SHIFTS, 2, CLASSES, ANGLES)
        scores = jnp.einsum('sekm,emp->skp', rounded, table_wide) * scale
        return lax.optimization_barrier(jnp.max(scores, axis=(0, 2)))
    best_scores = lax.map(score_one, jnp.transpose(particles, (1, 0, 2, 3)))
    valid_mask = jnp.arange(SIGNIF, dtype=jnp.int32)[None, :] < counts[:, None]
    kept = jnp.where(valid_mask, weights.astype(jnp.float32), jnp.float32(0.0))
    class_hit = (class_ids[:, :, None] == jnp.arange(CLASSES, dtype=jnp.int32)[None, None, :]).astype(jnp.float32)
    shift_hit = (shift_ids[:, :, None] == jnp.arange(SHIFTS, dtype=jnp.int32)[None, None, :]).astype(jnp.float32)
    mixing = jnp.einsum('ij,ijk,ijs->isk', kept, class_hit, shift_hit).astype(jnp.bfloat16)
    mixing = mixing.reshape(PARTICLES * SHIFTS, CLASSES).astype(jnp.float32)
    flat_images = particles.reshape(ANGLES, PARTICLES * SHIFTS, 2 * CYCLES).astype(jnp.float32)
    class_sums = jnp.einsum('nk,mnc->mkc', mixing, flat_images)
    weight_sums = jnp.einsum('ij,ijk->k', kept, class_hit)
    class_means = class_sums / jnp.maximum(weight_sums, 1.0)[None, :, None]
    return (best_scores, class_means)
```

```python
import functools
import math

import jax
import jax.numpy as jnp
from jax import lax
from jax.experimental import pallas as pl
from jax.experimental.pallas import tpu as pltpu
from jax.sharding import PartitionSpec as P

VMEM_LIMIT = 56 * 1024 * 1024


def up(value, unit):
    return -(-value // unit) * unit


def half_table(angles):
    rows = angles // 2 + 1
    padded = up(rows, 8)
    rotation = jnp.arange(padded, dtype=jnp.int32)
    rotation = jnp.where(rotation < rows, rotation, 0)
    product = rotation[:, None] * jnp.arange(angles, dtype=jnp.int32)[None, :] % angles
    phase_angle = product.astype(jnp.float32) * (2.0 * math.pi / angles)
    return jnp.concatenate([jnp.cos(phase_angle), -jnp.sin(phase_angle)]).astype(jnp.bfloat16)


def score_kernel(dims, x_ref, w_ref, t_ref, out_ref, held):
    groups, each, shifts, angles, chunk, slots, kpad, scale = dims
    rows = each * shifts
    step = pl.program_id(1)
    first = step * chunk

    def quad(index, carry):
        blocks = [
            x_ref[c, pl.ds(pl.multiple_of(index * 4 * rows, 16), 4 * rows), :] for c in range(groups)
        ]
        for part in range(4):
            start = part * rows // 16 * 16
            offset = part * rows - start
            size = up(offset + rows, 16)
            skip = offset // 8 * 8
            lhs = jnp.concatenate([b[start : start + size] for b in blocks], axis=0)
            prod = lax.dot_general(
                lhs, w_ref[index * 4 + part], (((1,), (1,)), ((), ())), preferred_element_type=jnp.float32
            )
            keep = up(offset - skip + rows, 8)
            slot = 8 - (offset - skip)
            for c in range(groups):
                value = prod[c * size + skip : c * size + skip + keep]
                begin = (c * slots + slot) * angles + first + index * 4 + part
                held[pl.ds(begin, keep, stride=angles), :] = value
        return carry

    lax.fori_loop(0, chunk // 4, quad, 0, unroll=2)

    @pl.when(step == pl.num_programs(1) - 1)
    def _():
        table = t_ref[...]
        half = table.shape[0] // 2
        width = 2 * kpad

        for c in range(groups):

            def one_shift(s, best):
                best = list(best)
                for pair in range(0, each, 2):
                    cols = []
                    for i in (pair, pair + 1):
                        at = pl.multiple_of((c * slots + 8 + s * each + i) * angles, angles)
                        cols.append(held[pl.ds(at, angles), :].astype(jnp.bfloat16))
                    both = jnp.dot(table, jnp.concatenate(cols, axis=1), preferred_element_type=jnp.float32)
                    for h in range(2):
                        even = both[:half, h * width : (h + 1) * width]
                        odd = pltpu.roll(both[half:, h * width : (h + 1) * width], kpad, 1)
                        total = even + jnp.abs(odd)
                        top = jnp.max(total.reshape(half // 8, 8, width), axis=0)
                        best[pair + h] = jnp.maximum(best[pair + h], top)
                return tuple(best)

            start = tuple(jnp.full((8, width), -jnp.inf, jnp.float32) for _ in range(each))
            best = lax.fori_loop(0, shifts, one_shift, start)
            for i in range(each):
                out_ref[c * each + i : c * each + i + 1, :] = jnp.max(best[i], axis=0, keepdims=True) * scale


def score(images, weights_of, table, each, shifts):
    all_groups = images.shape[0]
    groups = math.gcd(all_groups, 4)
    angles, width, parts = weights_of.shape
    rows = each * shifts
    chunk = 32
    slots = up(rows + 16, 4)
    scale = 1.0 / math.sqrt(float(parts * angles))
    dims = (groups, each, shifts, angles, chunk, slots, width // 2, scale)
    return pl.pallas_call(
        functools.partial(score_kernel, dims),
        out_shape=jax.ShapeDtypeStruct((all_groups * each, width), jnp.float32),
        grid=(all_groups // groups, angles // chunk),
        in_specs=[
            pl.BlockSpec((groups, chunk * rows, parts), lambda b, g: (b, g, 0)),
            pl.BlockSpec((chunk, width, parts), lambda b, g: (g, 0, 0)),
            pl.BlockSpec(table.shape, lambda b, g: (0, 0)),
        ],
        out_specs=pl.BlockSpec((groups * each, width), lambda b, g: (b, 0)),
        scratch_shapes=[pltpu.VMEM((groups * slots * angles, width), jnp.float32)],
        compiler_params=pltpu.CompilerParams(vmem_limit_bytes=VMEM_LIMIT),
        name="score",
    )(images, weights_of, table)


def mean_kernel(block, own, x_ref, s_ref, d_ref, out_ref):
    many = x_ref.shape[0]
    parts = x_ref.shape[2]
    classes = d_ref.shape[0]
    weights = s_ref[...]
    scale = d_ref[...]

    def body(index, carry):
        rows = x_ref[:, pl.ds(pl.multiple_of(index * block, 16), block), :].reshape(many * block, parts)
        sums = jnp.dot(weights, rows, preferred_element_type=jnp.float32)
        for part in range(4):
            value = sums[part * classes : (part + 1) * classes] / scale
            out_ref[pl.ds(index * 4 + part, classes, stride=own), :] = value
        return carry

    lax.fori_loop(0, own // 4, body, 0)


def on_device(particles, references, class_ids, counts, shift_ids, weights):
    dom_size = lax.axis_size("dom")
    cls_size = lax.axis_size("cls")
    cls_index = lax.axis_index("cls")
    angles, class_count, parts = references.shape
    cycles = parts // 2
    each, shifts = particles.shape[1:3]
    length = class_ids.shape[1]
    own = angles // dom_size

    ordered = jnp.transpose(particles, (0, 2, 1, 3))
    images = lax.all_gather(ordered.reshape(angles * shifts * each, parts), "cls", axis=0)

    valid = jnp.arange(length, dtype=jnp.int32)[None, :] < counts[:, None]
    kept = jnp.where(valid, weights.astype(jnp.float32), 0.0)
    packed = jnp.stack([class_ids.astype(jnp.float32).T, kept.T])
    listing = lax.all_gather(packed, ("dom", "cls"), axis=0)

    shift_of = shift_ids.T[None, :, :, None]
    chosen = jnp.broadcast_to(ordered[:, 0:1], (angles, length, each, parts))
    for s in range(1, shifts):
        chosen = jnp.where(shift_of == s, ordered[:, s : s + 1], chosen)
    sent = chosen.reshape(dom_size, own * length * each, parts)
    received = lax.all_to_all(sent, "dom", split_axis=0, concat_axis=0, tiled=True)
    received = lax.all_gather(received, "cls", axis=0)
    received = received.reshape(cls_size * dom_size, own * length * each, parts)

    kpad = up(class_count, 64)
    swapped = jnp.concatenate([-references[:, :, cycles:], references[:, :, :cycles]], axis=2)
    margin = ((0, 0), (0, kpad - class_count), (0, 0))
    stacked = jnp.concatenate([jnp.pad(references, margin), jnp.pad(swapped, margin)], axis=1)
    best = score(images, stacked, half_table(angles), each, shifts)[:, :class_count]

    listing = listing.reshape(dom_size, cls_size, 2, length * each).transpose(2, 1, 0, 3)
    local = listing[0].reshape(-1, length * each) - (cls_index * class_count).astype(jnp.float32)
    kept_all = listing[1].reshape(-1, length * each)
    mine = local[None] == jnp.arange(class_count, dtype=jnp.int32).astype(jnp.float32)[:, None, None]
    picked = jnp.where(mine, kept_all[None], 0.0)
    totals = jnp.maximum(jnp.sum(picked, axis=(1, 2)), 1.0)
    kept_rows = up(class_count, 8)
    picked = jnp.pad(picked, ((0, kept_rows - class_count), (0, 0), (0, 0))).astype(jnp.bfloat16)
    totals = jnp.pad(totals, (0, kept_rows - class_count), constant_values=1.0)
    many = cls_size * dom_size
    spread = jnp.eye(4, dtype=jnp.bfloat16)[:, None, None, :, None] * picked[None, :, :, None, :]
    block = 4 * length * each
    spread = spread.reshape(4 * kept_rows, many * block)
    means = pl.pallas_call(
        functools.partial(mean_kernel, block, own),
        out_shape=jax.ShapeDtypeStruct((kept_rows * own, parts), jnp.float32),
        in_specs=[pl.BlockSpec(memory_space=pltpu.VMEM)] * 3,
        out_specs=pl.BlockSpec(memory_space=pltpu.VMEM),
        compiler_params=pltpu.CompilerParams(vmem_limit_bytes=VMEM_LIMIT),
        name="means",
    )(received, spread, jnp.broadcast_to(totals[:, None], (kept_rows, parts)))
    means = means.reshape(kept_rows, own, parts)[:class_count]
    return (best, jnp.transpose(means, (1, 0, 2)))


def solution(mesh):
    return jax.shard_map(
        on_device,
        mesh=mesh,
        in_specs=(
            P(None, ("dom", "cls"), None, None),
            P(None, "cls", None),
            P(("dom", "cls"), None),
            P(("dom", "cls")),
            P(("dom", "cls"), None),
            P(("dom", "cls"), None),
        ),
        out_specs=(P("dom", "cls"), P("dom", "cls", None)),
        check_vma=False,
    )
```

```python
import functools
import math

import jax
import jax.numpy as jnp
from jax import lax
from jax.experimental import pallas as pl
from jax.experimental.pallas import tpu as pltpu
from jax.sharding import PartitionSpec as P

VMEM_LIMIT = 56 * 1024 * 1024


def up(value, unit):
    return -(-value // unit) * unit


def half_table(angles):
    rows = angles // 2 + 1
    padded = up(rows, 8)
    rotation = jnp.arange(padded, dtype=jnp.int32)
    rotation = jnp.where(rotation < rows, rotation, 0)
    product = rotation[:, None] * jnp.arange(angles, dtype=jnp.int32)[None, :] % angles
    phase_angle = product.astype(jnp.float32) * (2.0 * math.pi / angles)
    return jnp.concatenate([jnp.cos(phase_angle), -jnp.sin(phase_angle)]).astype(jnp.bfloat16)


def score_kernel(dims, *refs):
    groups, each, shifts, angles, chunk, slots, kpad, scale = dims
    x_refs = refs[:groups]
    w_ref, t_ref, out_ref, held = refs[groups:]
    stride = angles + 8
    rows = each * shifts
    step = pl.program_id(0)
    first = step * chunk

    def quad(index, carry):
        blocks = [
            ref[pl.ds(pl.multiple_of(index * 4 * rows, 16), 4 * rows), :] for ref in x_refs
        ]
        for part in range(4):
            start = part * rows // 16 * 16
            offset = part * rows - start
            size = up(offset + rows, 16)
            skip = offset // 8 * 8
            lhs = jnp.concatenate([b[start : start + size] for b in blocks], axis=0)
            prod = lax.dot_general(
                lhs, w_ref[index * 4 + part], (((1,), (1,)), ((), ())), preferred_element_type=jnp.float32
            )
            keep = up(offset - skip + rows, 8)
            slot = 8 - (offset - skip)
            for c in range(groups):
                value = prod[c * size + skip : c * size + skip + keep]
                begin = (c * slots + slot) * stride + first + index * 4 + part
                held[pl.ds(begin, keep, stride=stride), :] = value
        return carry

    lax.fori_loop(0, chunk // 4, quad, 0, unroll=2)

    @pl.when(step == pl.num_programs(0) - 1)
    def _():
        table = t_ref[...]
        half = table.shape[0] // 2
        width = 2 * kpad

        for c in range(groups):

            def one_shift(s, best):
                best = list(best)
                for pair in range(0, each, 2):
                    cols = []
                    for i in (pair, pair + 1):
                        at = pl.multiple_of((c * slots + 8 + s * each + i) * stride, 8)
                        cols.append(held[pl.ds(at, angles), :].astype(jnp.bfloat16))
                    both = jnp.dot(table, jnp.concatenate(cols, axis=1), preferred_element_type=jnp.float32)
                    for h in range(2):
                        even = both[:half, h * width : (h + 1) * width]
                        odd = pltpu.roll(both[half:, h * width : (h + 1) * width], kpad, 1)
                        total = even + jnp.abs(odd)
                        top = jnp.max(total.reshape(half // 8, 8, width), axis=0)
                        best[pair + h] = jnp.maximum(best[pair + h], top)
                return tuple(best)

            start = tuple(jnp.full((8, width), -jnp.inf, jnp.float32) for _ in range(each))
            best = lax.fori_loop(0, shifts, one_shift, start)
            for i in range(each):
                out_ref[c * each + i : c * each + i + 1, :] = jnp.max(best[i], axis=0, keepdims=True) * scale


def score(images, weights_of, table, each, shifts):
    groups = len(images)
    angles, width, parts = weights_of.shape
    rows = each * shifts
    chunk = 32
    slots = up(rows + 16, 4)
    scale = 1.0 / math.sqrt(float(parts * angles))
    dims = (groups, each, shifts, angles, chunk, slots, width // 2, scale)
    return pl.pallas_call(
        functools.partial(score_kernel, dims),
        out_shape=jax.ShapeDtypeStruct((groups * each, width), jnp.float32),
        grid=(angles // chunk,),
        in_specs=[
            *[pl.BlockSpec((chunk * rows, parts), lambda g: (g, 0))] * groups,
            pl.BlockSpec((chunk, width, parts), lambda g: (g, 0, 0)),
            pl.BlockSpec(table.shape, lambda g: (0, 0)),
        ],
        out_specs=pl.BlockSpec((groups * each, width), lambda g: (0, 0)),
        scratch_shapes=[pltpu.VMEM((groups * slots * (angles + 8), width), jnp.float32)],
        compiler_params=pltpu.CompilerParams(vmem_limit_bytes=VMEM_LIMIT),
        cost_estimate=pl.CostEstimate(
            flops=groups * angles * 2**25, bytes_accessed=groups * angles * rows * parts * 2, transcendentals=0
        ),
        name="score",
    )(*images, weights_of, table)


def mean_kernel(block, own, *refs):
    *x_refs, s_ref, d_ref, out_ref = refs
    many = x_refs[0].shape[0]
    parts = x_refs[0].shape[2]
    classes = d_ref.shape[0]
    weights = s_ref[...]
    scale = d_ref[...]

    def body(index, carry):
        at = pl.ds(pl.multiple_of(index * block, 16), block)
        rows = jnp.concatenate([ref[:, at, :].reshape(many * block, parts) for ref in x_refs], axis=0)
        sums = jnp.dot(weights, rows, preferred_element_type=jnp.float32)
        for part in range(4):
            value = sums[part * classes : (part + 1) * classes] / scale
            out_ref[pl.ds(index * 4 + part, classes, stride=own), :] = value
        return carry

    lax.fori_loop(0, own // 4, body, 0)


def swap(value, axis, mask):
    return lax.ppermute(value, axis, [(i, i ^ mask) for i in range(lax.axis_size(axis))])


def reorder(value, order, axis):
    value = jnp.moveaxis(value, axis, 0)
    hit = order[:, None] == jnp.arange(value.shape[0], dtype=jnp.int32)[None, :]
    hit = hit.reshape(hit.shape + (1,) * (value.ndim - 1))
    return jnp.moveaxis(jnp.sum(jnp.where(hit, value[None], 0.0), axis=1), 0, axis)


def gather_shards(value):
    shards = {0: value}
    bit = lax.axis_size("cls") // 2
    while bit:
        for mask in sorted(shards):
            shards[mask | bit] = swap(shards[mask], "cls", bit)
        bit //= 2
    return [shards[mask] for mask in sorted(shards)]


def on_device(particles, references, class_ids, counts, shift_ids, weights):
    dom_size = lax.axis_size("dom")
    cls_size = lax.axis_size("cls")
    cls_index = lax.axis_index("cls")
    dom_index = lax.axis_index("dom")
    cls_order = jnp.arange(cls_size, dtype=jnp.int32) ^ cls_index
    dom_order = jnp.arange(dom_size, dtype=jnp.int32) ^ dom_index
    angles, class_count, parts = references.shape
    cycles = parts // 2
    each, shifts = particles.shape[1:3]
    length = class_ids.shape[1]
    own = angles // dom_size

    ordered = jnp.transpose(particles, (0, 2, 1, 3))
    flat = ordered.reshape(angles * shifts * each, parts)

    valid = jnp.arange(length, dtype=jnp.int32)[None, :] < counts[:, None]
    kept = jnp.where(valid, weights.astype(jnp.float32), 0.0)
    packed = jnp.stack([class_ids.astype(jnp.float32).T, kept.T])
    listing = lax.all_gather(packed, ("dom", "cls"), axis=0)

    shift_of = shift_ids.T[None, :, :, None]
    chosen = jnp.broadcast_to(ordered[:, 0:1], (angles, length, each, parts))
    for s in range(1, shifts):
        chosen = jnp.where(shift_of == s, ordered[:, s : s + 1], chosen)
    sent = chosen.reshape(dom_size, own * length * each, parts)
    arrived = []
    for mask in range(dom_size):
        piece = lax.dynamic_index_in_dim(sent, dom_index ^ mask, 0, keepdims=True)
        arrived.append(swap(piece, "dom", mask) if mask else piece)
    received = gather_shards(jnp.concatenate(arrived, axis=0))

    kpad = up(class_count, 64)
    swapped = jnp.concatenate([-references[:, :, cycles:], references[:, :, :cycles]], axis=2)
    margin = ((0, 0), (0, kpad - class_count), (0, 0))
    stacked = jnp.concatenate([jnp.pad(references, margin), jnp.pad(swapped, margin)], axis=1)
    table = half_table(angles)
    bit, far = cls_size // 2, [flat]
    while bit > 1:
        far = far + [swap(shard, "cls", bit) for shard in far]
        bit //= 2
    best = [score([flat, swap(flat, "cls", 1)], stacked, table, each, shifts)]
    rest = far[1:]
    *rest, best[0] = lax.optimization_barrier((*rest, best[0]))
    best = best + [score([shard, swap(shard, "cls", 1)], stacked, table, each, shifts) for shard in rest]
    *received, best[-1] = lax.optimization_barrier((*received, best[-1]))
    masks = [0]
    bit = cls_size // 2
    while bit > 1:
        masks = masks + [mask | bit for mask in masks]
        bit //= 2
    best = [best[masks.index(mask)] for mask in sorted(masks)]
    best = jnp.concatenate(best, axis=0)[:, :class_count].reshape(cls_size, each, class_count)
    best = reorder(best, cls_order, 0).reshape(cls_size * each, class_count)

    listing = listing.reshape(dom_size, cls_size, 2, length * each).transpose(2, 1, 0, 3)
    listing = reorder(reorder(listing, cls_order, 1), dom_order, 2)
    local = listing[0].reshape(-1, length * each) - (cls_index * class_count).astype(jnp.float32)
    kept_all = listing[1].reshape(-1, length * each)
    mine = local[None] == jnp.arange(class_count, dtype=jnp.int32).astype(jnp.float32)[:, None, None]
    picked = jnp.where(mine, kept_all[None], 0.0)
    totals = jnp.maximum(jnp.sum(picked, axis=(1, 2)), 1.0)
    kept_rows = up(class_count, 8)
    picked = jnp.pad(picked, ((0, kept_rows - class_count), (0, 0), (0, 0))).astype(jnp.bfloat16)
    totals = jnp.pad(totals, (0, kept_rows - class_count), constant_values=1.0)
    many = cls_size * dom_size
    spread = jnp.eye(4, dtype=jnp.bfloat16)[:, None, None, :, None] * picked[None, :, :, None, :]
    block = 4 * length * each
    spread = spread.reshape(4 * kept_rows, many * block)
    means = pl.pallas_call(
        functools.partial(mean_kernel, block, own),
        out_shape=jax.ShapeDtypeStruct((kept_rows * own, parts), jnp.float32),
        in_specs=[pl.BlockSpec(memory_space=pltpu.VMEM)] * (cls_size + 2),
        out_specs=pl.BlockSpec(memory_space=pltpu.VMEM),
        compiler_params=pltpu.CompilerParams(vmem_limit_bytes=VMEM_LIMIT),
        name="means",
    )(*received, spread, jnp.broadcast_to(totals[:, None], (kept_rows, parts)))
    means = means.reshape(kept_rows, own, parts)[:class_count]
    return (best, jnp.transpose(means, (1, 0, 2)))


def solution(mesh):
    return jax.shard_map(
        on_device,
        mesh=mesh,
        in_specs=(
            P(None, ("dom", "cls"), None, None),
            P(None, "cls", None),
            P(("dom", "cls"), None),
            P(("dom", "cls")),
            P(("dom", "cls"), None),
            P(("dom", "cls"), None),
        ),
        out_specs=(P("dom", "cls"), P("dom", "cls", None)),
        check_vma=False,
    )
```

```python
import functools
import math

import jax
import jax.numpy as jnp
from jax import lax
from jax.experimental import pallas as pl
from jax.experimental.pallas import tpu as pltpu
from jax.sharding import PartitionSpec as P

VMEM_LIMIT = 56 * 1024 * 1024


def up(value, unit):
    return -(-value // unit) * unit


def half_table(angles):
    rows = angles // 2 + 1
    padded = up(rows, 8)
    rotation = jnp.arange(padded, dtype=jnp.int32)
    rotation = jnp.where(rotation < rows, rotation, 0)
    product = rotation[:, None] * jnp.arange(angles, dtype=jnp.int32)[None, :] % angles
    phase_angle = product.astype(jnp.float32) * (2.0 * math.pi / angles)
    return jnp.concatenate([jnp.cos(phase_angle), -jnp.sin(phase_angle)]).astype(jnp.bfloat16)


def score_kernel(dims, *refs):
    groups, each, shifts, angles, chunk, slots, kpad, scale = dims
    x_refs = refs[:groups]
    w_ref, t_ref, out_ref, held = refs[groups:]
    stride = angles + 8
    rows = each * shifts
    step = pl.program_id(0)
    first = step * chunk

    def quad(index, carry):
        blocks = [
            ref[pl.ds(pl.multiple_of(index * 4 * rows, 16), 4 * rows), :] for ref in x_refs
        ]
        for part in range(4):
            start = part * rows // 16 * 16
            offset = part * rows - start
            size = up(offset + rows, 16)
            skip = offset // 8 * 8
            lhs = jnp.concatenate([b[start : start + size] for b in blocks], axis=0)
            prod = lax.dot_general(
                lhs, w_ref[index * 4 + part], (((1,), (1,)), ((), ())), preferred_element_type=jnp.float32
            )
            keep = up(offset - skip + rows, 8)
            slot = 8 - (offset - skip)
            for c in range(groups):
                value = prod[c * size + skip : c * size + skip + keep]
                begin = (c * slots + slot) * stride + first + index * 4 + part
                held[pl.ds(begin, keep, stride=stride), :] = value
        return carry

    lax.fori_loop(0, chunk // 4, quad, 0, unroll=2)

    @pl.when(step == pl.num_programs(0) - 1)
    def _():
        table = t_ref[...]
        half = table.shape[0] // 2
        width = 2 * kpad

        for c in range(groups):

            def one_shift(s, best):
                best = list(best)
                for pair in range(0, each, 2):
                    cols = []
                    for i in (pair, pair + 1):
                        at = pl.multiple_of((c * slots + 8 + s * each + i) * stride, 8)
                        cols.append(held[pl.ds(at, angles), :].astype(jnp.bfloat16))
                    both = jnp.dot(table, jnp.concatenate(cols, axis=1), preferred_element_type=jnp.float32)
                    for h in range(2):
                        even = both[:half, h * width : (h + 1) * width]
                        odd = pltpu.roll(both[half:, h * width : (h + 1) * width], kpad, 1)
                        total = even + jnp.abs(odd)
                        top = jnp.max(total.reshape(half // 8, 8, width), axis=0)
                        best[pair + h] = jnp.maximum(best[pair + h], top)
                return tuple(best)

            start = tuple(jnp.full((8, width), -jnp.inf, jnp.float32) for _ in range(each))
            best = lax.fori_loop(0, shifts, one_shift, start)
            for i in range(each):
                out_ref[c * each + i : c * each + i + 1, :] = jnp.max(best[i], axis=0, keepdims=True) * scale


def score(images, weights_of, table, each, shifts):
    groups = len(images)
    angles, width, parts = weights_of.shape
    rows = each * shifts
    chunk = 32
    slots = up(rows + 16, 4)
    scale = 1.0 / math.sqrt(float(parts * angles))
    dims = (groups, each, shifts, angles, chunk, slots, width // 2, scale)
    return pl.pallas_call(
        functools.partial(score_kernel, dims),
        out_shape=jax.ShapeDtypeStruct((groups * each, width), jnp.float32),
        grid=(angles // chunk,),
        in_specs=[
            *[pl.BlockSpec((chunk * rows, parts), lambda g: (g, 0))] * groups,
            pl.BlockSpec((chunk, width, parts), lambda g: (g, 0, 0)),
            pl.BlockSpec(table.shape, lambda g: (0, 0)),
        ],
        out_specs=pl.BlockSpec((groups * each, width), lambda g: (0, 0)),
        scratch_shapes=[pltpu.VMEM((groups * slots * (angles + 8), width), jnp.float32)],
        compiler_params=pltpu.CompilerParams(vmem_limit_bytes=VMEM_LIMIT),
        cost_estimate=pl.CostEstimate(
            flops=groups * angles * 2**25, bytes_accessed=groups * angles * rows * parts * 2, transcendentals=0
        ),
        name="score",
    )(*images, weights_of, table)


def mean_kernel(block, own, *refs):
    *x_refs, s_ref, d_ref, out_ref = refs
    many = x_refs[0].shape[0]
    parts = x_refs[0].shape[2]
    classes = out_ref.shape[0] // own
    pitch = d_ref.shape[0]
    weights = s_ref[...]
    scale = d_ref[:classes]

    def body(index, carry):
        at = pl.ds(pl.multiple_of(index * block, 16), block)
        rows = jnp.concatenate([ref[:, at, :].reshape(many * block, parts) for ref in x_refs], axis=0)
        sums = jnp.dot(weights, rows, preferred_element_type=jnp.float32)
        for part in range(4):
            value = sums[part * pitch : part * pitch + classes] / scale
            out_ref[pl.ds(index * 4 + part, classes, stride=own), :] = value
        return carry

    lax.fori_loop(0, own // 4, body, 0)


def swap(value, axis, mask):
    return lax.ppermute(value, axis, [(i, i ^ mask) for i in range(lax.axis_size(axis))])


def reorder(value, order, axis):
    value = jnp.moveaxis(value, axis, 0)
    hit = order[:, None] == jnp.arange(value.shape[0], dtype=jnp.int32)[None, :]
    hit = hit.reshape(hit.shape + (1,) * (value.ndim - 1))
    return jnp.moveaxis(jnp.sum(jnp.where(hit, value[None], 0.0), axis=1), 0, axis)


def on_device(particles, references, class_ids, counts, shift_ids, weights):
    dom_size = lax.axis_size("dom")
    cls_size = lax.axis_size("cls")
    cls_index = lax.axis_index("cls")
    dom_index = lax.axis_index("dom")
    cls_order = jnp.arange(cls_size, dtype=jnp.int32) ^ cls_index
    angles, class_count, parts = references.shape
    cycles = parts // 2
    each, shifts = particles.shape[1:3]
    length = class_ids.shape[1]
    own = angles // dom_size

    ordered = jnp.transpose(particles, (0, 2, 1, 3))
    flat = ordered.reshape(angles * shifts * each, parts)

    valid = jnp.arange(length, dtype=jnp.int32)[None, :] < counts[:, None]
    kept = jnp.where(valid, weights, jnp.zeros_like(weights)).T.reshape(1, length * each)
    ids = class_ids.T.reshape(1, length * each)
    packed = jnp.concatenate([kept, (ids // 32).astype(jnp.bfloat16), (ids % 32).astype(jnp.bfloat16)], axis=0)
    packed = jnp.pad(packed, ((0, 16 - packed.shape[0]), (0, parts - length * each)))

    shift_of = shift_ids.T[None, :, :, None]
    chosen = jnp.broadcast_to(ordered[:, 0:1], (angles, length, each, parts))
    for s in range(1, shifts):
        chosen = jnp.where(shift_of == s, ordered[:, s : s + 1], chosen)
    sent = chosen.reshape(dom_size, own * length * each, parts)
    sent = jnp.concatenate([sent, jnp.broadcast_to(packed[None], (dom_size, 16, parts))], axis=1)
    arrived = []
    for mask in range(dom_size):
        piece = lax.dynamic_index_in_dim(sent, dom_index ^ mask, 0, keepdims=True)
        arrived.append(swap(piece, "dom", mask) if mask else piece)
    received = jnp.concatenate(arrived, axis=0)

    kpad = up(class_count, 64)
    swapped = jnp.concatenate([-references[:, :, cycles:], references[:, :, :cycles]], axis=2)
    margin = ((0, 0), (0, kpad - class_count), (0, 0))
    stacked = jnp.concatenate([jnp.pad(references, margin), jnp.pad(swapped, margin)], axis=1)
    table = half_table(angles)
    bit, far = cls_size // 2, [flat]
    while bit > 1:
        far = far + [swap(shard, "cls", bit) for shard in far]
        bit //= 2
    near, received, stacked, table = lax.optimization_barrier((swap(flat, "cls", 1), received, stacked, table))
    best = [score([flat, near], stacked, table, each, shifts)]
    bit, lists = cls_size // 2, [received]
    while bit > 1:
        lists = lists + [swap(listed, "cls", bit) for listed in lists]
        bit //= 2
    rest = far[1:]
    *rest, best[0], lists = lax.optimization_barrier((*rest, best[0], lists))
    received = [entry for listed in lists for entry in (listed, swap(listed, "cls", 1))]
    best = best + [score([shard, swap(shard, "cls", 1)], stacked, table, each, shifts) for shard in rest]
    *received, best[-1] = lax.optimization_barrier((*received, best[-1]))
    masks = [0]
    bit = cls_size // 2
    while bit > 1:
        masks = masks + [mask | bit for mask in masks]
        bit //= 2
    best = [best[masks.index(mask)] for mask in sorted(masks)]
    best = jnp.concatenate(best, axis=0)[:, :class_count].reshape(cls_size, each, class_count)
    best = reorder(best, cls_order, 0).reshape(cls_size * each, class_count)

    listing = jnp.concatenate([entry[:, own * length * each :][:, :3, : length * each] for entry in received])
    listing = listing.astype(jnp.float32)
    kept_all = listing[:, 0]
    local = listing[:, 1] * 32.0 + listing[:, 2] - (cls_index * class_count).astype(jnp.float32)
    mine = local[None] == jnp.arange(class_count, dtype=jnp.int32).astype(jnp.float32)[:, None, None]
    picked = jnp.where(mine, kept_all[None], 0.0)
    totals = jnp.maximum(jnp.sum(picked, axis=(1, 2)), 1.0)
    kept_rows = up(class_count, 8)
    picked = jnp.pad(picked, ((0, kept_rows - class_count), (0, 0), (0, 0))).astype(jnp.bfloat16)
    totals = jnp.pad(totals, (0, kept_rows - class_count), constant_values=1.0)
    many = cls_size * dom_size
    spread = jnp.eye(4, dtype=jnp.bfloat16)[:, None, None, :, None] * picked[None, :, :, None, :]
    block = 4 * length * each
    spread = spread.reshape(4 * kept_rows, many * block)
    means = pl.pallas_call(
        functools.partial(mean_kernel, block, own),
        out_shape=jax.ShapeDtypeStruct((class_count * own, parts), jnp.float32),
        in_specs=[pl.BlockSpec(memory_space=pltpu.VMEM)] * (cls_size + 2),
        out_specs=pl.BlockSpec(memory_space=pltpu.VMEM),
        compiler_params=pltpu.CompilerParams(vmem_limit_bytes=VMEM_LIMIT),
        name="means",
    )(*received, spread, jnp.broadcast_to(totals[:, None], (kept_rows, parts)))
    means = means.reshape(class_count, own, parts)
    return (best, jnp.transpose(means, (1, 0, 2)))


def solution(mesh):
    return jax.shard_map(
        on_device,
        mesh=mesh,
        in_specs=(
            P(None, ("dom", "cls"), None, None),
            P(None, "cls", None),
            P(("dom", "cls"), None),
            P(("dom", "cls")),
            P(("dom", "cls"), None),
            P(("dom", "cls"), None),
        ),
        out_specs=(P("dom", "cls"), P("dom", "cls", None)),
        check_vma=False,
    )
```
